32 devices in a mesh: lon: 16 (over z, y, x), ch: 2 (over core).
Axes of the slice: x: 2, y: 2, z: 4, core: 2. Of those that a mesh axis runs over, the one named last changes fastest.
Arguments:
- coarse: bfloat16 [16, 4, 64, 1024], P(None, None, 'lon', 'ch'), may hold values from -6 to 6
- up_kernel: bfloat16 [4, 4, 1024, 512], P(None, None, 'ch', 'lon'), may hold values from -0.09375 to 0.09375
- up_bias: float32 [512], replicated, may hold values from -3 to 3
- conv_kernel: bfloat16 [3, 3, 512, 512], P(None, None, 'lon'), may hold values from -0.09375 to 0.09375
- conv_bias: float32 [512], replicated, may hold values from -3 to 3
Outputs:
- fine_out: bfloat16 [32, 4, 128, 512], P('ch', None, 'lon')
The draws below stay inside these ranges and needn't reach their ends.
All inputs are finite; a program needn't handle non-finite values.
Results may differ from the reference program's by a relative error of at most 0.015.
Values may be sent and summed in bfloat16 or wider, within the bound.
No kernel may reach another device: no remote copies, remote signals or barrier semaphores. Data moves between devices by JAX's collectives and lax.ppermute only.
A program may use at most 64 MiB of HBM per device.

```python
import jax
import jax.numpy as jnp
from jax import lax

CIN = 1024
COUT = 512
BATCH = 4
LAT = 16
LONC = 64
LATF = 32
LONF = 128
N_CH = 2


def steps_of(own_key, extent, split, low, largest):
    loudness, own = 1.0, jax.random.fold_in(own_key, 6)
    for dim, blocks in split:
        draws = jnp.exp(jax.random.uniform(jax.random.fold_in(own, dim), (blocks,), jnp.float32, low / len(split), largest / len(split)))
        loudness = loudness * jnp.repeat(draws, extent[dim] // blocks).reshape([-1 if axis == dim else 1 for axis in range(len(extent))])
    return loudness


def centred(rng, extent, deviation, bound, cuts=(), dtype=jnp.bfloat16):
    level = steps_of(rng, extent, cuts, -0.22, 0.18) if cuts else 1.0
    array = jax.random.normal(rng, extent, jnp.float32) * deviation * level
    return jnp.minimum(jnp.maximum(array, -bound), bound).astype(dtype)


def setup_inputs(seed: int = 0) -> dict:
    key_of = jax.random.split(jax.random.key(seed), 6)
    return {
        "coarse": centred(key_of[0], (LAT, BATCH, LONC, CIN), 1.0, 6.0, ((2, 16), (3, 2))),
        "up_kernel": centred(key_of[1], (4, 4, CIN, COUT), (4 * CIN) ** -0.5, 0.09375, ((2, 2), (3, 16))),
        "up_bias": centred(key_of[2], (COUT,), 0.5, 3.0, (), jnp.float32),
        "conv_kernel": centred(key_of[3], (3, 3, COUT, COUT), (9 * COUT) ** -0.5, 0.09375, ((2, 16),)),
        "conv_bias": centred(key_of[4], (COUT,), 0.5, 3.0, (), jnp.float32),
    }


TAPS = (((1, 1), (3, 0)), ((2, 1), (0, 2)))


def tap_dot(piece, weight):
    flat = piece.reshape(-1, piece.shape[-1])
    result = jnp.dot(flat, weight, preferred_element_type=jnp.float32)
    return result.reshape(piece.shape[:-1] + (weight.shape[-1],))


def upsample(padded, lon_count, weights):
    rows = padded.shape[0] - 2
    batch = padded.shape[1]
    phases = []
    for p in range(2):
        columns = []
        for q in range(2):
            total = None
            for a, row_off in TAPS[p]:
                for c, col_off in TAPS[q]:
                    piece = padded[row_off:row_off + rows, :, col_off:col_off + lon_count, :]
                    term = tap_dot(piece, weights[a, c])
                    total = term if total is None else total + term
            columns.append(total)
        phases.append(jnp.stack(columns, axis=3))
    stacked = jnp.stack(phases, axis=1)
    return stacked.reshape(2 * rows, batch, 2 * lon_count, weights.shape[-1])


def reference(coarse, up_kernel, up_bias, conv_kernel, conv_bias):
    block = CIN // N_CH

    def add_block(k, total):
        start = (k * block).astype(jnp.int32)
        piece = lax.dynamic_slice_in_dim(coarse, start, block, 3)
        kernel = lax.dynamic_slice_in_dim(up_kernel, start, block, 2)
        padded = jnp.pad(piece, ((1, 1), (0, 0), (0, 0), (0, 0)))
        padded = jnp.concatenate([padded[:, :, -1:], padded, padded[:, :, :1]], axis=2)
        partial_value = upsample(padded, LONC, kernel).astype(jnp.bfloat16)
        return total + partial_value.astype(jnp.float32)

    total = jnp.zeros((LATF, BATCH, LONF, COUT), jnp.float32)
    total = lax.fori_loop(0, N_CH, add_block, total)
    hidden = jax.nn.gelu(total + up_bias, approximate=False).astype(jnp.bfloat16)
    padded = jnp.pad(hidden, ((1, 1), (0, 0), (0, 0), (0, 0)))
    padded = jnp.concatenate([padded[:, :, -1:], padded, padded[:, :, :1]], axis=2)
    result = jnp.zeros((LATF, BATCH, LONF, COUT), jnp.float32) + conv_bias
    for d in range(3):
        for t in range(3):
            result = result + tap_dot(padded[d:d + LATF, :, t:t + LONF, :], conv_kernel[d, t])
    return result.astype(jnp.bfloat16)
```

```python
import functools

import jax
import jax.numpy as jnp
from jax import lax
from jax.experimental import pallas as pl
from jax.experimental.pallas import tpu as pltpu
from jax.sharding import PartitionSpec as P

TAPS = (((1, 1), (3, 0)), ((2, 1), (0, 2)))
FRAME_COST = 0
PACK_COST = 0
SPLIT = 12
VMEM_LIMIT = 16 * 1024 * 1024
X, Y, Z0, Z1 = 1, 2, 4, 8


def padded_2(block, sides, width, periodic):
    for axis, dim in sides:
        count = lax.axis_size(axis)
        forward = [(i, i + 1) for i in range(count - 1)]
        if periodic:
            forward.append((count - 1, 0))
        backward = [(target, source) for source, target in forward]
        low = lax.ppermute(
            lax.slice_in_dim(block, block.shape[dim] - width, None, axis=dim), axis, forward
        )
        high = lax.ppermute(lax.slice_in_dim(block, 0, width, axis=dim), axis, backward)
        block = jnp.concatenate([low, block, high], axis=dim)
    return block


def tap_dot(piece, weight):
    return jnp.einsum("rbjc,cn->rbjn", piece, weight, preferred_element_type=jnp.float32)


def upsample(padded, lon_count, weights):
    rows = padded.shape[0] - 2
    batch = padded.shape[1]
    phases = []
    for p in range(2):
        columns = []
        for q in range(2):
            total = None
            for a, row_off in TAPS[p]:
                for c, col_off in TAPS[q]:
                    piece = padded[row_off : row_off + rows, :, col_off : col_off + lon_count, :]
                    term = tap_dot(piece, weights[a, c])
                    total = term if total is None else total + term
            columns.append(total)
        phases.append(jnp.stack(columns, axis=3))
    stacked = jnp.stack(phases, axis=1)
    return stacked.reshape(2 * rows, batch, 2 * lon_count, weights.shape[-1])


def general_shards(coarse, up_kernel, up_bias, conv_kernel, conv_bias):
    lon_dev = coarse.shape[2]
    row_padded = jnp.pad(coarse, ((1, 1), (0, 0), (0, 0), (0, 0)))
    source = padded_2(row_padded, (("lon", 2),), 1, True)
    up_full = lax.all_gather(up_kernel, "lon", axis=3, tiled=True)
    partial_value = upsample(source, lon_dev, up_full)
    summed = lax.psum_scatter(
        partial_value.astype(jnp.bfloat16), "ch", scatter_dimension=0, tiled=True
    ).astype(jnp.float32)
    hidden = jax.nn.gelu(summed + up_bias, approximate=False).astype(jnp.bfloat16)
    widened = padded_2(hidden, (("lon", 2),), 1, True)
    framed = padded_2(widened, (("ch", 0),), 1, False)
    weights = lax.all_gather(conv_kernel, "lon", axis=2, tiled=True)
    band_rows = hidden.shape[0]
    fine_cols = hidden.shape[2]
    result = jnp.zeros(hidden.shape, jnp.float32) + conv_bias
    for d in range(3):
        for t in range(3):
            result = result + tap_dot(
                framed[d : d + band_rows, :, t : t + fine_cols, :], weights[d, t]
            )
    return result.astype(jnp.bfloat16)


def slot_of(lon):
    return (lon // Y) % 4


def group_of(lon):
    return lon % 2 + 2 * (lon // Z1)


def exchange(block, bits):
    return lax.ppermute(block, "lon", [(i, i ^ bits) for i in range(lax.axis_size("lon"))])


def swap_cores(block):
    return lax.ppermute(block, "ch", [(0, 1), (1, 0)])


def pack_body(place, *refs):
    packed = refs[3]
    width = refs[0].shape[1]
    group = 4 * width
    slot = slot_of(place[1])
    for j, taps in enumerate(refs[:3]):
        offset = pl.multiple_of(jnp.bitwise_xor(slot, j) * width, width)
        for a in range(4):
            for c in range(4):
                row = (2 * (a % 2) + c % 2) * group + offset
                packed[1 - a // 2, 1 - c // 2, pl.ds(row, width), :] = taps[4 * a + c]


def pack_last_body(place, first, second, begun, packed):
    width = first.shape[1]
    group = 4 * width
    offset = pl.multiple_of(jnp.bitwise_xor(slot_of(place[1]), 3) * width, width)
    for a in range(4):
        for c in range(4):
            tap = 4 * a + c
            block = first[tap] if tap < SPLIT else second[tap - SPLIT]
            row = (2 * (a % 2) + c % 2) * group + offset
            packed[1 - a // 2, 1 - c // 2, pl.ds(row, width), :] = block


def up_body(geo, place, *refs):
    rows, batch, own = geo
    pairs, halos, packed, out_ref = (refs[0:2], refs[2:4]), refs[4:6], refs[6], refs[7]
    low, high = refs[8:]
    side, right = place[0] if own else 1 - place[0], place[1] % 2
    band = rows // 2
    edge = jnp.zeros(low.shape[2:], low.dtype)
    spare = jnp.zeros((batch, low.shape[3]), low.dtype)

    @pl.loop(0, band + 2)
    def _(n):
        row = side * band + n - 1
        inside = jnp.logical_and(row >= 0, row < rows)

        @pl.when(inside)
        def _():
            for s, (mine, partner) in enumerate(pairs):
                a, b, c, d = halos[s][0, row], mine[row], partner[row], halos[s][1, row]
                line = jnp.where(
                    right == 0,
                    jnp.concatenate([a, b, c, d], axis=0),
                    jnp.concatenate([d, c, b, a], axis=0),
                )
                low[s, n] = line
                high[s, n] = jnp.concatenate([line[batch:], spare], axis=0)

        @pl.when(jnp.logical_not(inside))
        def _():
            for s in range(2):
                low[s, n] = edge
                high[s, n] = edge

    for s in range(2):
        total = None
        for dy in range(2):
            for dx, shifted in enumerate((low, high)):
                left = shifted[s, dy : dy + band + 1].reshape(-1, low.shape[3])
                term = lax.dot_general(
                    left, packed[dy, dx], (((1,), (1,)), ((), ())), preferred_element_type=jnp.float32
                )
                total = term if total is None else total + term
        out_ref[s] = total.reshape(out_ref.shape[1:]).astype(out_ref.dtype)


def hidden_body(batch, place, *refs):
    owns, others, bias_ref, outs = refs[0], refs[1], refs[2], refs[3:]
    core, right = place[0], place[1] % 2
    cell = outs[0].shape[1]
    half = outs[0].shape[2] // 2
    last = outs[0].shape[0] - 1
    shift = cell - batch

    @pl.loop(0, last + 1)
    def _(i):
        for s in range(2):
            v = owns[s, i].astype(jnp.float32) + others[s, i].astype(jnp.float32) + bias_ref[...]
            h = v * (1.0 + lax.erf(v * 0.7071067811865476)) * 0.5
            h = h.astype(jnp.bfloat16)
            first, second = h[:cell], h[shift : shift + cell]
            outs[2 * s][i] = jnp.where(right == 0, first, second)
            outs[2 * s + 1][i] = jnp.where(right == 0, second, first)

    for out in outs:

        @pl.when(core == 0)
        def _():
            out[0, :, 0:half] = jnp.zeros((cell, half), jnp.bfloat16)

        @pl.when(core == 1)
        def _():
            out[last, :, half:] = jnp.zeros((cell, half), jnp.bfloat16)


def frame_body(geo, place, *refs):
    batch, hops = geo
    pieces, shifted = refs[: len(hops)], refs[len(hops)]
    span = shifted.shape[2]
    group = pieces[0].shape[2] // 4
    for piece, bits in zip(pieces, hops):
        source = jnp.bitwise_xor(place[1], bits)
        offset = pl.multiple_of(group_of(source) * group, group)
        for i in range(piece.shape[0]):
            for p in range(2):
                for q in range(2):
                    lane = (2 * p + q) * group
                    block = piece[i, :, lane : lane + group]
                    shifted[2 * i + p, q, :, pl.ds(offset, group)] = block[0:span]
                    shifted[2 * i + p, 2 + q, :, pl.ds(offset, group)] = block[batch : batch + span]


def conv_body(geo, place, *refs):
    batch, blocks = geo
    shifted, mine, others = refs[0], refs[1 : 1 + len(blocks)], refs[1 + len(blocks) : 1 + 2 * len(blocks)]
    bias_ref, out_ref, packed, total_ref, natural = refs[1 + 2 * len(blocks) :]
    core, me = place[0], place[1]
    rows, _, fine, cout = out_ref.shape
    cols = fine // 2
    span = cols * batch
    width = mine[0].shape[2]
    group = 4 * width
    half = mine[0].shape[-1]
    for sources, side in ((mine, core), (others, 1 - core)):
        lanes = pl.ds(pl.multiple_of(side * half, half), half)
        for ref, owners in zip(sources, blocks):
            for n, bits in enumerate(owners):
                source = jnp.bitwise_xor(me, bits)
                start = group_of(source) * group + slot_of(source) * width
                start = pl.multiple_of(start, width)
                for tap in range(9):
                    packed[tap, pl.ds(start, width), lanes] = ref[n, tap]
    total = None
    for d in range(3):
        for t in range(3):
            left = shifted[d : d + rows, t : t + 2].reshape(rows * 2 * span, -1)
            term = jnp.dot(left, packed[3 * d + t], preferred_element_type=jnp.float32)
            total = term if total is None else total + term
    total = (total + bias_ref[...]).reshape(rows, 2, span, -1)
    for n in range(total_ref.shape[0]):
        lanes = slice(n * 128, (n + 1) * 128)
        total_ref[n] = total[..., lanes]
        for r in range(rows):
            for c in range(2):
                for b in range(batch):
                    natural[n, r, b, pl.ds(c, cols, stride=2), :] = total_ref[
                        n, r, c, pl.ds(b, cols, stride=batch), :
                    ]
        out_ref[:, :, :, lanes] = natural[n].astype(out_ref.dtype)


def local_call(body, outs, scratch, flops, *args, aliases={}):
    specs = [pl.BlockSpec(memory_space=pltpu.SMEM)]
    specs += [pl.BlockSpec(memory_space=pltpu.VMEM)] * (len(args) - 1)
    return pl.pallas_call(
        body,
        out_shape=outs,
        in_specs=specs,
        out_specs=[pl.BlockSpec(memory_space=pltpu.VMEM)] * len(outs),
        scratch_shapes=scratch,
        input_output_aliases=aliases,
        compiler_params=pltpu.CompilerParams(vmem_limit_bytes=VMEM_LIMIT),
        cost_estimate=pl.CostEstimate(flops=flops, bytes_accessed=8 << 20, transcendentals=0),
    )(*args)


def grouped_shards(coarse, up_kernel, up_bias, conv_kernel, conv_bias):
    rows, batch, cols, depth = coarse.shape
    width = up_kernel.shape[3]
    cout = conv_kernel.shape[3]
    group = 4 * width
    half = cout // 2
    band = rows // 2
    line = 2 * (cols + 1) * batch
    cell = (cols + 1) * batch
    core, me, lon = lax.axis_index("ch"), lax.axis_index("lon"), lax.axis_size("lon")
    place = jnp.stack([core, me]).astype(jnp.int32)

    taps = up_kernel.transpose(0, 1, 3, 2).reshape(16, width, depth)
    taps_z = exchange(taps, Z0)
    taps_y = exchange(taps, Y)
    edge = lax.dynamic_slice_in_dim(coarse, (cols - 1) * (me % 2), 1, 2)
    halos = [
        lax.ppermute(
            edge, "lon", [(i, (i + (step if i % 2 else -step)) % lon) for i in range(lon)]
        ).reshape(rows, batch, depth)
        for step in (1, 2)
    ]
    piece = coarse.transpose(0, 2, 1, 3).reshape(rows, cols * batch, depth)
    near = exchange(piece, X)
    far = exchange(piece, Z1)
    kernel, _ = lax.optimization_barrier((conv_kernel, halos))
    part = lax.dynamic_slice_in_dim(kernel.reshape(9, width, cout), core * half, half, 2)
    part_z = exchange(part, Z1)
    bias = up_bias.reshape(2, 4, 2, width)
    bias = lax.dynamic_slice_in_dim(bias, me // Z1, 1, 0)
    bias = lax.dynamic_slice_in_dim(bias, me % 2, 1, 2)
    bias = jnp.tile(bias.reshape(1, group), (1, 4))
    far, near, taps_y, taps_z, bias, place = lax.optimization_barrier(
        (far, near, taps_y, taps_z, bias, place)
    )
    far_near = exchange(far, X)
    halos = jnp.stack(halos)
    far_halos = exchange(halos, Z1)
    packed_shape = jax.ShapeDtypeStruct((2, 2, 4 * group, depth), jnp.bfloat16)
    (begun,) = local_call(pack_body, [packed_shape], [], PACK_COST, place, taps, taps_y, taps_z)
    taps_zy = [exchange(taps_z[:SPLIT], Y), exchange(taps_y[SPLIT:], Z0)]
    two = jnp.stack([part, part_z])
    two_z = exchange(two, Z0)

    (packed,) = local_call(
        pack_last_body, [packed_shape], [], 0, place, *taps_zy, begun, aliases={3: 0}
    )
    sums = jax.ShapeDtypeStruct((2, band + 1, line, 4 * group), jnp.bfloat16)
    chunk = jax.ShapeDtypeStruct((band + 1, cell, 4 * group), jnp.bfloat16)

    def up(own, packed):
        return local_call(
            functools.partial(up_body, (rows, batch, own)),
            [sums],
            [pltpu.VMEM((2, band + 2, line, depth), jnp.bfloat16)] * 2,
            2 * 2 * (band + 1) * line * 4 * depth * 4 * group,
            place,
            far,
            far_near,
            piece,
            near,
            far_halos,
            halos,
            packed,
        )

    (given,) = up(False, packed)
    arrived = swap_cores(given)
    packed, _ = lax.optimization_barrier((packed, given))
    (kept,) = up(True, packed)
    far_same, far_across, near_same, near_across = local_call(
        functools.partial(hidden_body, batch),
        [chunk] * 4,
        [],
        2 * 40 * (band + 1) * line * 4 * group,
        place,
        kept,
        arrived,
        bias,
    )
    four = jnp.concatenate([two, two_z])
    four_x, four_y, _ = lax.optimization_barrier((exchange(four, X), exchange(four, Y), far_same))
    low_xy = exchange(four_y[:2], X)
    high_xy = exchange(four_x[2:], Y)
    order = (0, Z1, Z0, Z0 | Z1)
    mine = [four, four_x, four_y, low_xy, high_xy]
    owners = (
        order,
        tuple(m ^ X for m in order),
        tuple(m ^ Y for m in order),
        tuple(m ^ X ^ Y for m in order[:2]),
        tuple(m ^ X ^ Y for m in order[2:]),
    )
    others = [swap_cores(block) for block in mine]
    hops = (0, X, Z1, X | Z1)
    pieces = [
        near_same,
        exchange(near_across, X),
        exchange(far_same, Z1),
        exchange(far_across, X | Z1),
    ]
    (framed,) = local_call(
        functools.partial(frame_body, (batch, hops)),
        [jax.ShapeDtypeStruct((rows + 2, 4, cols * batch, cout), jnp.bfloat16)],
        [],
        FRAME_COST,
        place,
        *pieces,
    )
    (result,) = local_call(
        functools.partial(conv_body, (batch, owners)),
        [jax.ShapeDtypeStruct((rows, batch, 2 * cols, cout), jnp.bfloat16)],
        [
            pltpu.VMEM((9, cout, cout), jnp.bfloat16),
            pltpu.VMEM((cout // 128, rows, 2, cols * batch, 128), jnp.float32),
            pltpu.VMEM((cout // 128, rows, batch, 2 * cols, 128), jnp.float32),
        ],
        2 * rows * 2 * cols * batch * 9 * cout * cout,
        place,
        framed,
        *mine,
        *others,
        conv_bias.reshape(1, cout),
    )
    return result


def solution(mesh):
    lon, ch = mesh.shape["lon"], mesh.shape["ch"]

    def shards(coarse, up_kernel, up_bias, conv_kernel, conv_bias):
        fits = (
            ch == 2
            and lon == 16
            and 4 * up_kernel.shape[3] == 128
            and coarse.shape[1] * coarse.shape[2] == 16
        )
        plan = grouped_shards if fits else general_shards
        return plan(coarse, up_kernel, up_bias, conv_kernel, conv_bias)

    return jax.shard_map(
        shards,
        mesh=mesh,
        in_specs=(
            P(None, None, "lon", "ch"),
            P(None, None, "ch", "lon"),
            P(),
            P(None, None, "lon", None),
            P(),
        ),
        out_specs=P("ch", None, "lon", None),
        check_vma=False,
    )
```

```python
import functools

import jax
import jax.numpy as jnp
from jax import lax
from jax.experimental import pallas as pl
from jax.experimental.pallas import tpu as pltpu
from jax.sharding import PartitionSpec as P

TAPS = (((1, 1), (3, 0)), ((2, 1), (0, 2)))
FRAME_COST = 0
PACK_COST = 0
SPLIT = 8
VMEM_LIMIT = 16 * 1024 * 1024
X, Y, Z0, Z1 = 1, 2, 4, 8


def padded_2(block, sides, width, periodic):
    for axis, dim in sides:
        count = lax.axis_size(axis)
        forward = [(i, i + 1) for i in range(count - 1)]
        if periodic:
            forward.append((count - 1, 0))
        backward = [(target, source) for source, target in forward]
        low = lax.ppermute(
            lax.slice_in_dim(block, block.shape[dim] - width, None, axis=dim), axis, forward
        )
        high = lax.ppermute(lax.slice_in_dim(block, 0, width, axis=dim), axis, backward)
        block = jnp.concatenate([low, block, high], axis=dim)
    return block


def tap_dot(piece, weight):
    return jnp.einsum("rbjc,cn->rbjn", piece, weight, preferred_element_type=jnp.float32)


def upsample(padded, lon_count, weights):
    rows = padded.shape[0] - 2
    batch = padded.shape[1]
    phases = []
    for p in range(2):
        columns = []
        for q in range(2):
            total = None
            for a, row_off in TAPS[p]:
                for c, col_off in TAPS[q]:
                    piece = padded[row_off : row_off + rows, :, col_off : col_off + lon_count, :]
                    term = tap_dot(piece, weights[a, c])
                    total = term if total is None else total + term
            columns.append(total)
        phases.append(jnp.stack(columns, axis=3))
    stacked = jnp.stack(phases, axis=1)
    return stacked.reshape(2 * rows, batch, 2 * lon_count, weights.shape[-1])


def general_shards(coarse, up_kernel, up_bias, conv_kernel, conv_bias):
    lon_dev = coarse.shape[2]
    row_padded = jnp.pad(coarse, ((1, 1), (0, 0), (0, 0), (0, 0)))
    source = padded_2(row_padded, (("lon", 2),), 1, True)
    up_full = lax.all_gather(up_kernel, "lon", axis=3, tiled=True)
    partial_value = upsample(source, lon_dev, up_full)
    summed = lax.psum_scatter(
        partial_value.astype(jnp.bfloat16), "ch", scatter_dimension=0, tiled=True
    ).astype(jnp.float32)
    hidden = jax.nn.gelu(summed + up_bias, approximate=False).astype(jnp.bfloat16)
    widened = padded_2(hidden, (("lon", 2),), 1, True)
    framed = padded_2(widened, (("ch", 0),), 1, False)
    weights = lax.all_gather(conv_kernel, "lon", axis=2, tiled=True)
    band_rows = hidden.shape[0]
    fine_cols = hidden.shape[2]
    result = jnp.zeros(hidden.shape, jnp.float32) + conv_bias
    for d in range(3):
        for t in range(3):
            result = result + tap_dot(
                framed[d : d + band_rows, :, t : t + fine_cols, :], weights[d, t]
            )
    return result.astype(jnp.bfloat16)


def slot_of(lon):
    return (lon // Y) % 4


def group_of(lon):
    return lon % 2 + 2 * (lon // Z1)


def exchange(block, bits):
    return lax.ppermute(block, "lon", [(i, i ^ bits) for i in range(lax.axis_size("lon"))])


def swap_cores(block):
    return lax.ppermute(block, "ch", [(0, 1), (1, 0)])


def pack_body(place, *refs):
    packed = refs[3]
    width = refs[0].shape[1]
    group = 4 * width
    slot = slot_of(place[1])
    for j, taps in enumerate(refs[:3]):
        offset = pl.multiple_of(jnp.bitwise_xor(slot, j) * width, width)
        for a in range(4):
            for c in range(4):
                row = (2 * (a % 2) + c % 2) * group + offset
                packed[1 - a // 2, 1 - c // 2, pl.ds(row, width), :] = taps[4 * a + c]


def pack_last_body(place, first, second, begun, packed):
    width = first.shape[1]
    group = 4 * width
    offset = pl.multiple_of(jnp.bitwise_xor(slot_of(place[1]), 3) * width, width)
    for a in range(4):
        for c in range(4):
            tap = 4 * a + c
            block = first[tap] if tap < SPLIT else second[tap - SPLIT]
            row = (2 * (a % 2) + c % 2) * group + offset
            packed[1 - a // 2, 1 - c // 2, pl.ds(row, width), :] = block


def up_body(geo, place, *refs):
    rows, batch, own = geo
    pairs, halos, packed, out_ref = (refs[0:2], refs[2:4]), refs[4:6], refs[6], refs[7]
    low, high = refs[8:]
    side, right = place[0] if own else 1 - place[0], place[1] % 2
    band = rows // 2
    edge = jnp.zeros(low.shape[2:], low.dtype)
    spare = jnp.zeros((batch, low.shape[3]), low.dtype)

    @pl.loop(0, band + 2)
    def _(n):
        row = side * band + n - 1
        inside = jnp.logical_and(row >= 0, row < rows)

        @pl.when(inside)
        def _():
            for s, (mine, partner) in enumerate(pairs):
                a, b, c, d = halos[s][0, row], mine[row], partner[row], halos[s][1, row]
                line = jnp.where(
                    right == 0,
                    jnp.concatenate([a, b, c, d], axis=0),
                    jnp.concatenate([d, c, b, a], axis=0),
                )
                low[s, n] = line
                high[s, n] = jnp.concatenate([line[batch:], spare], axis=0)

        @pl.when(jnp.logical_not(inside))
        def _():
            for s in range(2):
                low[s, n] = edge
                high[s, n] = edge

    for s in range(2):
        total = None
        for dy in range(2):
            for dx, shifted in enumerate((low, high)):
                left = shifted[s, dy : dy + band + 1].reshape(-1, low.shape[3])
                term = lax.dot_general(
                    left, packed[dy, dx], (((1,), (1,)), ((), ())), preferred_element_type=jnp.float32
                )
                total = term if total is None else total + term
        out_ref[s] = total.reshape(out_ref.shape[1:]).astype(out_ref.dtype)


def hidden_body(batch, place, *refs):
    owns, others, bias_ref, outs = refs[0], refs[1], refs[2], refs[3:]
    core, right = place[0], place[1] % 2
    cell = outs[0].shape[1]
    half = outs[0].shape[2] // 2
    last = outs[0].shape[0] - 1
    shift = cell - batch

    @pl.loop(0, last + 1)
    def _(i):
        for s in range(2):
            v = owns[s, i].astype(jnp.float32) + others[s, i].astype(jnp.float32) + bias_ref[...]
            h = v * (1.0 + lax.erf(v * 0.7071067811865476)) * 0.5
            h = h.astype(jnp.bfloat16)
            first, second = h[:cell], h[shift : shift + cell]
            outs[2 * s][i] = jnp.where(right == 0, first, second)
            outs[2 * s + 1][i] = jnp.where(right == 0, second, first)

    for out in outs:

        @pl.when(core == 0)
        def _():
            out[0, :, 0:half] = jnp.zeros((cell, half), jnp.bfloat16)

        @pl.when(core == 1)
        def _():
            out[last, :, half:] = jnp.zeros((cell, half), jnp.bfloat16)


def frame_body(geo, place, *refs):
    batch, hops = geo
    pieces, shifted = refs[: len(hops)], refs[len(hops)]
    span = shifted.shape[2]
    group = pieces[0].shape[2] // 4
    for piece, bits in zip(pieces, hops):
        source = jnp.bitwise_xor(place[1], bits)
        offset = pl.multiple_of(group_of(source) * group, group)
        for i in range(piece.shape[0]):
            for p in range(2):
                for q in range(2):
                    lane = (2 * p + q) * group
                    block = piece[i, :, lane : lane + group]
                    shifted[2 * i + p, q, :, pl.ds(offset, group)] = block[0:span]
                    shifted[2 * i + p, 2 + q, :, pl.ds(offset, group)] = block[batch : batch + span]


def conv_body(geo, place, *refs):
    batch, blocks = geo
    shifted, mine, others = refs[0], refs[1 : 1 + len(blocks)], refs[1 + len(blocks) : 1 + 2 * len(blocks)]
    bias_ref, out_ref, packed, total_ref, natural = refs[1 + 2 * len(blocks) :]
    core, me = place[0], place[1]
    rows, _, fine, cout = out_ref.shape
    cols = fine // 2
    span = cols * batch
    width = mine[0].shape[2]
    group = 4 * width
    half = mine[0].shape[-1]
    for sources, side in ((mine, core), (others, 1 - core)):
        lanes = pl.ds(pl.multiple_of(side * half, half), half)
        for ref, owners in zip(sources, blocks):
            for n, bits in enumerate(owners):
                source = jnp.bitwise_xor(me, bits)
                start = group_of(source) * group + slot_of(source) * width
                start = pl.multiple_of(start, width)
                for tap in range(9):
                    packed[tap, pl.ds(start, width), lanes] = ref[n, tap]
    total = None
    for d in range(3):
        for t in range(3):
            left = shifted[d : d + rows, t : t + 2].reshape(rows * 2 * span, -1)
            term = jnp.dot(left, packed[3 * d + t], preferred_element_type=jnp.float32)
            total = term if total is None else total + term
    total = (total + bias_ref[...]).reshape(rows, 2, span, -1)
    for n in range(total_ref.shape[0]):
        lanes = slice(n * 128, (n + 1) * 128)
        total_ref[n] = total[..., lanes]
        for r in range(rows):
            for c in range(2):
                for b in range(batch):
                    natural[n, r, b, pl.ds(c, cols, stride=2), :] = total_ref[
                        n, r, c, pl.ds(b, cols, stride=batch), :
                    ]
        out_ref[:, :, :, lanes] = natural[n].astype(out_ref.dtype)


def local_call(body, outs, scratch, flops, *args, aliases={}):
    specs = [pl.BlockSpec(memory_space=pltpu.SMEM)]
    specs += [pl.BlockSpec(memory_space=pltpu.VMEM)] * (len(args) - 1)
    return pl.pallas_call(
        body,
        out_shape=outs,
        in_specs=specs,
        out_specs=[pl.BlockSpec(memory_space=pltpu.VMEM)] * len(outs),
        scratch_shapes=scratch,
        input_output_aliases=aliases,
        compiler_params=pltpu.CompilerParams(vmem_limit_bytes=VMEM_LIMIT),
        cost_estimate=pl.CostEstimate(flops=flops, bytes_accessed=8 << 20, transcendentals=0),
    )(*args)


def grouped_shards(coarse, up_kernel, up_bias, conv_kernel, conv_bias):
    rows, batch, cols, depth = coarse.shape
    width = up_kernel.shape[3]
    cout = conv_kernel.shape[3]
    group = 4 * width
    half = cout // 2
    band = rows // 2
    line = 2 * (cols + 1) * batch
    cell = (cols + 1) * batch
    core, me, lon = lax.axis_index("ch"), lax.axis_index("lon"), lax.axis_size("lon")
    place = jnp.stack([core, me]).astype(jnp.int32)

    taps = up_kernel.transpose(0, 1, 3, 2).reshape(16, width, depth)
    taps_z = exchange(taps, Z0)
    taps_y = exchange(taps, Y)
    edge = lax.dynamic_slice_in_dim(coarse, (cols - 1) * (me % 2), 1, 2)
    halos = [
        lax.ppermute(
            edge, "lon", [(i, (i + (step if i % 2 else -step)) % lon) for i in range(lon)]
        ).reshape(rows, batch, depth)
        for step in (1, 2)
    ]
    piece = coarse.transpose(0, 2, 1, 3).reshape(rows, cols * batch, depth)
    near = exchange(piece, X)
    far = exchange(piece, Z1)
    kernel, _ = lax.optimization_barrier((conv_kernel, halos))
    part = lax.dynamic_slice_in_dim(kernel.reshape(9, width, cout), core * half, half, 2)
    part_z = exchange(part, Z1)
    bias = up_bias.reshape(2, 4, 2, width)
    bias = lax.dynamic_slice_in_dim(bias, me // Z1, 1, 0)
    bias = lax.dynamic_slice_in_dim(bias, me % 2, 1, 2)
    bias = jnp.tile(bias.reshape(1, group), (1, 4))
    far, near, taps_y, taps_z, bias, place = lax.optimization_barrier(
        (far, near, taps_y, taps_z, bias, place)
    )
    far_near = exchange(far, X)
    halos = jnp.stack(halos)
    far_halos = exchange(halos, Z1)
    packed_shape = jax.ShapeDtypeStruct((2, 2, 4 * group, depth), jnp.bfloat16)
    (begun,) = local_call(pack_body, [packed_shape], [], PACK_COST, place, taps, taps_y, taps_z)
    taps_zy = [exchange(taps_z[:SPLIT], Y), exchange(taps_y[SPLIT:], Z0)]
    two = jnp.stack([part, part_z])
    two_z = exchange(two, Z0)

    (packed,) = local_call(
        pack_last_body, [packed_shape], [], 0, place, *taps_zy, begun, aliases={3: 0}
    )
    sums = jax.ShapeDtypeStruct((2, band + 1, line, 4 * group), jnp.bfloat16)
    chunk = jax.ShapeDtypeStruct((band + 1, cell, 4 * group), jnp.bfloat16)

    def up(own, packed):
        return local_call(
            functools.partial(up_body, (rows, batch, own)),
            [sums],
            [pltpu.VMEM((2, band + 2, line, depth), jnp.bfloat16)] * 2,
            2 * 2 * (band + 1) * line * 4 * depth * 4 * group,
            place,
            far,
            far_near,
            piece,
            near,
            far_halos,
            halos,
            packed,
        )

    (given,) = up(False, packed)
    arrived = swap_cores(given)
    packed, _ = lax.optimization_barrier((packed, given))
    (kept,) = up(True, packed)
    far_same, far_across, near_same, near_across = local_call(
        functools.partial(hidden_body, batch),
        [chunk] * 4,
        [],
        2 * 40 * (band + 1) * line * 4 * group,
        place,
        kept,
        arrived,
        bias,
    )
    four = jnp.concatenate([two, two_z])
    four_x, four_y, _ = lax.optimization_barrier((exchange(four, X), exchange(four, Y), far_same))
    low_xy = exchange(four_y[:2], X)
    high_xy = exchange(four_x[2:], Y)
    order = (0, Z1, Z0, Z0 | Z1)
    mine = [four, four_x, four_y, low_xy, high_xy]
    owners = (
        order,
        tuple(m ^ X for m in order),
        tuple(m ^ Y for m in order),
        tuple(m ^ X ^ Y for m in order[:2]),
        tuple(m ^ X ^ Y for m in order[2:]),
    )
    others = [swap_cores(block) for block in mine]
    hops = (0, X, X | Z1, Z1)
    pieces = [
        near_same,
        exchange(near_across, X),
        exchange(far_across, X | Z1),
        exchange(far_same, Z1),
    ]
    (framed,) = local_call(
        functools.partial(frame_body, (batch, hops)),
        [jax.ShapeDtypeStruct((rows + 2, 4, cols * batch, cout), jnp.bfloat16)],
        [],
        FRAME_COST,
        place,
        *pieces,
    )
    (result,) = local_call(
        functools.partial(conv_body, (batch, owners)),
        [jax.ShapeDtypeStruct((rows, batch, 2 * cols, cout), jnp.bfloat16)],
        [
            pltpu.VMEM((9, cout, cout), jnp.bfloat16),
            pltpu.VMEM((cout // 128, rows, 2, cols * batch, 128), jnp.float32),
            pltpu.VMEM((cout // 128, rows, batch, 2 * cols, 128), jnp.float32),
        ],
        2 * rows * 2 * cols * batch * 9 * cout * cout,
        place,
        framed,
        *mine,
        *others,
        conv_bias.reshape(1, cout),
    )
    return result


def solution(mesh):
    lon, ch = mesh.shape["lon"], mesh.shape["ch"]

    def shards(coarse, up_kernel, up_bias, conv_kernel, conv_bias):
        fits = (
            ch == 2
            and lon == 16
            and 4 * up_kernel.shape[3] == 128
            and coarse.shape[1] * coarse.shape[2] == 16
        )
        plan = grouped_shards if fits else general_shards
        return plan(coarse, up_kernel, up_bias, conv_kernel, conv_bias)

    return jax.shard_map(
        shards,
        mesh=mesh,
        in_specs=(
            P(None, None, "lon", "ch"),
            P(None, None, "ch", "lon"),
            P(),
            P(None, None, "lon", None),
            P(),
        ),
        out_specs=P("ch", None, "lon", None),
        check_vma=False,
    )
```
